256 devices in a mesh: rel: 8 (over z_lo, core), ent: 32 (over x, z_hi, y).
Axes of the slice: x: 4, y: 4, z: 8 (z_hi: 2, z_lo: 4; z = z_hi * 4 + z_lo), core: 2. Of those that a mesh axis runs over, the one named last changes fastest.
Arguments:
- facts: bfloat16 [64, 4096, 4096], P('rel', 'ent'), may hold values from -6 to 6
- observed: int32 [64, 4096, 316], P('rel', 'ent'), may hold values from 0 to 8191
- factors: bfloat16 [4096, 128], P('ent'), may hold values from -0.59765625 to 0.59765625
- cores: bfloat16 [64, 128, 128], P('rel'), may hold values from -6 to 6
Outputs:
- grad_factors: float32 [4096, 128], P('ent')
- grad_cores: float32 [64, 128, 128], P('rel')
The draws below stay inside these ranges and needn't reach their ends.
All inputs are finite; a program needn't handle non-finite values.
Results may differ from the reference program's by a relative error of at most 0.0008.
Values may be sent and summed in bfloat16 or wider, within the bound.
A program may use at most 128 MiB of HBM per device.

```python
import jax
import jax.numpy as jnp
from jax import lax

R = 128
N = 4096
K = 64
WORDS = 316


def place_ends(drawn, own_key, least, largest):
    longest = drawn.shape.index(max(drawn.shape))
    spots = []
    for shift in (0, 1):
        where = [jax.random.randint(jax.random.fold_in(own_key, axis), (), 0, length) for axis, length in enumerate(drawn.shape)]
        where[longest] = (where[longest] + shift) % drawn.shape[longest]
        spots.append(tuple(where))
    return drawn.at[spots[0]].set(least).at[spots[1]].set(largest)


def spiked(array, key, source, target, shards_of, factor):
    owner, partner = [(jnp.arange(array.shape[axis_at]) // (array.shape[axis_at] // shards_of)).reshape([-1 if axis == axis_at else 1 for axis in range(array.ndim)]) for axis_at in (source, target)]
    chosen = jax.random.permutation(key, shards_of)[partner]
    strong = (owner == chosen) | (owner == (partner + shards_of // 2) % shards_of)
    return jnp.where(strong, factor * array, array)


def block_scale(rng, extent, split, smallest, top_value):
    gain, own = 1.0, jax.random.fold_in(rng, 6)
    for position, blocks in split:
        heights = jnp.exp(jax.random.uniform(jax.random.fold_in(own, position), (blocks,), jnp.float32, smallest / len(split), top_value / len(split)))
        gain = gain * jnp.repeat(heights, extent[position] // blocks).reshape([-1 if axis == position else 1 for axis in range(len(extent))])
    return gain


def bell_draw(key, dims, spread, bound, split=(), held_as=jnp.bfloat16):
    result = spread * jax.random.normal(key, dims, jnp.float32)
    if split:
        result = result * block_scale(key, dims, split, -0.22, 0.18)
    return jnp.clip(result, -bound, bound).astype(held_as)


def bell_draw_with(stream_key, dims, deviation, most, pieces, heavy, held_as=jnp.bfloat16):
    values = deviation * jax.random.normal(stream_key, dims, jnp.float32)
    if pieces:
        values = values * block_scale(stream_key, dims, pieces, -0.22, 0.18)
    return jnp.clip(spiked(values, jax.random.fold_in(stream_key, 3), *heavy), -most, most).astype(held_as)


def setup_inputs(seed: int = 0) -> dict:
    key_of = jax.random.split(jax.random.key(seed), 5)
    return {
        "facts": bell_draw_with(key_of[0], (K, N, N), 1.0, 6.0, ((0, 8), (1, 32)), (1, 2, 32, 2.75)),
        "observed": place_ends(jax.random.randint(key_of[1], (K, N, WORDS), 0, 8192), jax.random.fold_in(key_of[1], 1), 0, 8191).astype(jnp.int32),
        "factors": bell_draw(key_of[2], (N, R), 0.0884, 0.59765625, ((0, 32),)),
        "cores": bell_draw(key_of[3], (K, R, R), 1.0, 6.0, ((0, 8),)),
    }


def unpack(words, count):
    shifts = jnp.arange(13, dtype=jnp.int32)
    bits = jnp.bitwise_and(jnp.right_shift(words[..., None], shifts), 1)
    flat = bits.reshape(words.shape[:-1] + (words.shape[-1] * 13,))
    return flat[..., :count].astype(jnp.bfloat16)

def reference(facts, observed, factors, cores):

    def one_relation(items):
        data, words, core = items
        mask = unpack(words, N)
        left = jnp.dot(factors, core, preferred_element_type=jnp.float32).astype(jnp.bfloat16)
        right = jnp.dot(factors, core.T, preferred_element_type=jnp.float32).astype(jnp.bfloat16)
        model = jnp.dot(left, factors.T, preferred_element_type=jnp.float32)
        err = (mask.astype(jnp.float32) * (model - data.astype(jnp.float32))).astype(jnp.bfloat16)
        rows = jnp.dot(err, right, preferred_element_type=jnp.float32) + jnp.dot(err.T, left, preferred_element_type=jnp.float32)
        pull = jnp.dot(err, factors, preferred_element_type=jnp.float32).astype(jnp.bfloat16)
        core_grad = jnp.dot(factors.T, pull, preferred_element_type=jnp.float32)
        return (rows, core_grad)
    rows, core_grad = lax.map(one_relation, (facts, observed, cores))
    grad_factors = lax.optimization_barrier(jnp.sum(rows, axis=0)) / jnp.sqrt(jnp.float32(N * K))
    grad_cores = core_grad * (R / N)
    return (grad_factors, grad_cores)
```

```python
import math

import jax
import jax.numpy as jnp
from jax import lax
from jax.experimental import pallas as pl
from jax.experimental.pallas import tpu as pltpu
from jax.sharding import PartitionSpec as P

F32, BF16 = jnp.float32, jnp.bfloat16
MESH = pl.DeviceIdType.MESH
NT = (((1,), (1,)), ((), ()))
WIDE = BF16

COUNTS = dict(
    a1=3, z=2, a2=3, b1=3, b2=3, fwd=8, swap=8, r1=6, r2=6, zr=8, own=1, fin=1,
    k1=6, k2=6, k3=1, k4=6, k5=6,
)
BASE, TOTAL = {}, 0
for _name, _count in COUNTS.items():
    BASE[_name] = TOTAL
    TOTAL += _count


def unpack(obs_ref, mask_ref, k):
    words = obs_ref[k]
    n_words = words.shape[1]
    n_tiles = mask_ref.shape[2] // 128
    both = jnp.bitwise_or(words[0:64], jnp.left_shift(words[64:128], 16))
    sources = []
    for first in range(0, n_words, 128):
        part = both[:, first : first + 128]
        if part.shape[1] < 128:
            fill = jnp.zeros((64, 128 - part.shape[1]), jnp.int32)
            part = jnp.concatenate([part, fill], axis=1)
        sources.append(part)
    lane = lax.broadcasted_iota(jnp.int32, (64, 128), 1)
    for q in range(13):
        column = lane + 128 * q
        word = (column * 5042) >> 16
        low = jnp.left_shift(1, column - word * 13)
        high = jnp.left_shift(low, 16)
        for period, source in enumerate(sources):
            tile = 13 * period + q
            if tile >= n_tiles:
                continue
            spread = jnp.take_along_axis(source, word, axis=1, mode="promise_in_bounds")
            at = slice(128 * tile, 128 * tile + 128)
            mask_ref[k, 0:64, at] = jnp.where((spread & low) != 0, 1.0, 0.0).astype(BF16)
            mask_ref[k, 64:128, at] = jnp.where((spread & high) != 0, 1.0, 0.0).astype(BF16)


def kernel(
    facts_hbm, obs_hbm, fac_hbm, cores_hbm, gf_ref, gc_ref,
    facts, obs, fac, cores, mask, left, left_t, err, pull, pull_hi, spread_f,
    blk, swapped, acc, r1_out, r1_in, r2_in, ring, own, own_in, total, total_in,
    part, k1_in, k_sum, k2_in, k_small, k3_in, k_final,
    local, send, recv,
):
    rel, ent = lax.axis_index("rel"), lax.axis_index("ent")
    zl, h = rel // 2, rel % 2
    x, zh, y = ent // 8, (ent // 4) % 2, ent % 4
    z = zh * 4 + zl
    other = 1 - h

    def dev(x=x, y=y, zh=zh, zl=zl, c=h):
        return {"rel": zl * 2 + c, "ent": x * 8 + zh * 4 + y}

    xp = lambda d: (x + d + 4) % 4
    yp = lambda d: (y + d + 4) % 4
    sibling = dev(c=other)

    def message(kind, index, src, dst, to):
        at = BASE[kind] + index
        return pltpu.make_async_remote_copy(
            src_ref=src, dst_ref=dst, send_sem=send.at[at], recv_sem=recv.at[at],
            device_id=to, device_id_type=MESH,
        )

    def start(kind, index, src, dst, to):
        message(kind, index, src, dst, to).start()

    def arrive(kind, index, dst):
        message(kind, index, dst, dst, sibling).wait_recv()

    def sent(kind, index, src):
        message(kind, index, src, src, sibling).wait_send()

    loads = [
        pltpu.make_async_copy(fac_hbm, fac, local.at[0]),
        pltpu.make_async_copy(obs_hbm, obs, local.at[1]),
        pltpu.make_async_copy(cores_hbm, cores, local.at[2]),
        pltpu.make_async_copy(facts_hbm, facts, local.at[3]),
    ]
    for load in loads:
        load.start()
    barrier = pltpu.get_barrier_semaphore()
    greeted = (
        [dev(x=xp(d)) for d in (1, 2, 3)]
        + [dev(y=yp(d)) for d in (1, 2, 3)]
        + [dev(zh=(z + d) % 8 // 4, zl=(z + d) % 4) for d in range(1, 8)]
        + [sibling]
    )
    for device in greeted:
        pl.semaphore_signal(barrier, inc=1, device_id=device, device_id_type=MESH)

    loads[1].wait()

    def one_mask(k, carry):
        unpack(obs, mask, k)
        return carry

    lax.fori_loop(0, obs.shape[0], one_mask, 0)
    pull[...] = jnp.zeros_like(pull)
    loads[0].wait()
    half = pl.ds(pl.multiple_of(h * 64, 64), 64)
    other_half = pl.ds(pl.multiple_of(other * 64, 64), 64)
    spread_f[0, y, x, h] = fac[half, :]

    pl.semaphore_wait(barrier, len(greeted))

    for d in (1, 2, 3):
        start("a1", d - 1, fac.at[half, :], spread_f.at[0, y, x, h], dev(x=xp(d)))
    near = ((0, 3, 2), (3, 0, 1))
    for source, *targets in near:
        @pl.when(zl == source)
        def _():
            for i, target in enumerate(targets):
                start(
                    "z", i, fac.at[half, :], spread_f.at[1, x, y, h], dev(zh=1 - zh, zl=target)
                )

    loads[2].wait()
    for k in range(cores.shape[0]):
        rows = slice(128 * k, 128 * k + 128)
        value = jnp.dot(fac[...], cores[k], preferred_element_type=F32)
        left[rows, :] = value.astype(BF16)
        left_t[:, rows] = value.T.astype(BF16)

    for d in (1, 2, 3):
        arrive("a1", d - 1, spread_f.at[0, y, xp(-d), h])
    row = spread_f.at[0, y, :, h]
    for d in (1, 2, 3):
        start("a2", d - 1, row, row, dev(y=yp(d)))
    start("fwd", 0, row, row, sibling)
    for source, *targets in near:
        for i, target in enumerate(targets):
            @pl.when(zl == target)
            def _():
                arrive("z", i, spread_f.at[1, x, y, h])
    for d in (1, 2, 3):
        start("b1", d - 1, spread_f.at[1, x, y, h], spread_f.at[1, x, y, h], dev(y=yp(d)))
    loads[3].wait()

    column = spread_f.at[1, x, :, h]

    def place(t):
        third = (t + 1) // 3
        later = (third + 1) // 2
        part_of = (t % 2) * (1 - later) + third // 2
        d = later * ((t + 1) % 3 + 1)
        group = (y + part_of * (x - y) - d + 4) % 4
        return part_of, group

    def settle(t):
        part_of, group = place(t)
        arrive("swap", t, swapped.at[t])

        @pl.when(t < 2)
        def _():
            acc[part_of] = blk[t, half, :] + swapped[t]

        @pl.when(t >= 2)
        def _():
            r1_out[t - 2] = (blk[t, half, :] + swapped[t]).astype(r1_out.dtype)

        @pl.when((t >= 2) & (t < 5))
        def _():
            start("r1", t - 2, r1_out.at[t - 2], r1_in.at[t - 2], dev(y=group))

        @pl.when(t >= 5)
        def _():
            start("r1", t - 2, r1_out.at[t - 2], r1_in.at[t - 2], dev(x=group))

    def step(t, carry):
        part_of, group = place(t)

        @pl.when(t == 1)
        def _():
            for d in (1, 2, 3):
                arrive("b1", d - 1, spread_f.at[1, x, yp(-d), h])
            for d in (1, 2, 3):
                start("b2", d - 1, column, column, dev(x=xp(d)))
            start("fwd", 1, column, column, sibling)

        @pl.when(t == 2)
        def _():
            for d in (1, 2, 3):
                block = spread_f.at[0, yp(-d), :, h]
                arrive("a2", d - 1, block)
                start("fwd", 1 + d, block, block, sibling)

        @pl.when(t == 5)
        def _():
            for d in (1, 2, 3):
                block = spread_f.at[1, xp(-d), :, h]
                arrive("b2", d - 1, block)
                start("fwd", 4 + d, block, block, sibling)

        arrive("fwd", t, spread_f.at[part_of, group, :, other])
        rows = spread_f[part_of, group].reshape(512, 128)
        model = lax.dot_general(left[...], rows, NT, preferred_element_type=F32)
        for m in range(4):
            entity = (1 - part_of) * (m * 8 + zh * 4 + group) + part_of * (
                group * 8 + (1 - zh) * 4 + m
            )
            at = pl.ds(pl.multiple_of(entity * 128, 128), 128)
            for k in range(cores.shape[0]):
                here = slice(128 * k, 128 * k + 128)
                there = slice(128 * m, 128 * m + 128)
                diff = model[here, there] - facts[k, :, at].astype(F32)
                err[here, there] = diff.astype(BF16) * mask[k, :, at]
        pull[...] += jnp.dot(err[...], rows, preferred_element_type=F32)
        blk[t] = jnp.dot(left_t[...], err[...], preferred_element_type=F32)
        start("swap", t, blk.at[t, other_half, :], swapped.at[t], sibling)

        @pl.when(t >= 1)
        def _():
            settle(t - 1)

        return carry

    lax.fori_loop(0, 8, step, 0)

    fac_t = fac[...].astype(F32).T.astype(BF16)
    pull_hi[...] = pull[...].astype(BF16)
    for k in range(cores.shape[0]):
        rows = slice(128 * k, 128 * k + 128)
        part[k] = jnp.dot(fac_t, pull_hi[rows, :], preferred_element_type=F32)
    for d in (1, 2, 3):
        start("k1", d - 1, part.at[xp(d)], k1_in.at[d - 1], dev(x=xp(d)))
        start("k1", d + 2, part.at[4 + yp(d)], k1_in.at[d + 2], dev(y=yp(d)))
    own_value = jnp.zeros((128, 128), F32)
    for k in range(cores.shape[0]):
        rows = slice(128 * k, 128 * k + 128)
        high = pull_hi[rows, :]
        low = (pull[rows, :] - high.astype(F32)).astype(BF16)
        own_value += lax.dot_general(cores[k], high, NT, preferred_element_type=F32)
        own_value += lax.dot_general(cores[k], low, NT, preferred_element_type=F32)
    own[...] = own_value
    start("own", 0, own.at[other_half, :], own_in, sibling)
    settle(7)

    for d in range(6):
        arrive("k1", d, k1_in.at[d])
    k_sum[0] = part[x] + k1_in[0] + k1_in[1] + k1_in[2]
    k_sum[1] = part[4 + y] + k1_in[3] + k1_in[4] + k1_in[5]
    quarter = lambda i: pl.ds(pl.multiple_of(i * 32, 32), 32)
    for d in (1, 2, 3):
        start("k2", d - 1, k_sum.at[0, quarter(yp(d)), :], k2_in.at[d - 1], dev(y=yp(d)))
        start("k2", d + 2, k_sum.at[1, quarter(xp(d)), :], k2_in.at[d + 2], dev(x=xp(d)))

    for i in range(6):
        arrive("r1", i, r1_in.at[i])
    acc[0] = acc[0] + r1_in[0].astype(F32) + r1_in[1].astype(F32) + r1_in[2].astype(F32)
    acc[1] = acc[1] + r1_in[3].astype(F32) + r1_in[4].astype(F32) + r1_in[5].astype(F32)
    lanes = lambda i: pl.ds(pl.multiple_of(i * 128, 128), 128)
    for d in (1, 2, 3):
        start("r2", d - 1, acc.at[0, :, lanes(xp(d))], r2_in.at[d - 1], dev(x=xp(d)))
        start("r2", d + 2, acc.at[1, :, lanes(yp(d))], r2_in.at[d + 2], dev(y=yp(d)))

    for i in range(6):
        arrive("k2", i, k2_in.at[i])
    k_small[0, 0:32] = k_sum[0, quarter(y), :] + k2_in[0] + k2_in[1] + k2_in[2]
    k_small[0, 32:64] = k_sum[1, quarter(x), :] + k2_in[3] + k2_in[4] + k2_in[5]
    start("k3", 0, k_small.at[0], k3_in, dev(zh=1 - zh))

    arrive("own", 0, own_in)
    for i in range(6):
        arrive("r2", i, r2_in.at[i])
    ring[z] = (
        acc[0, :, lanes(x)] + r2_in[0] + r2_in[1] + r2_in[2] + own[half, :] + own_in[...]
    )
    total[0] = acc[1, :, lanes(y)] + r2_in[3] + r2_in[4] + r2_in[5]
    for d in (1, 2, 3):
        start("zr", d - 1, ring.at[z], ring.at[z], dev(zl=(zl + d) % 4))
    for d in range(4):
        start("zr", d + 3, total.at[0], ring.at[z], dev(zh=1 - zh, zl=(zl + d) % 4))

    n_all = facts.shape[2]
    n_rel = cores.shape[0] * lax.axis_size("rel")
    arrive("k3", 0, k3_in)
    k_small[1] = (k_small[0] + k3_in[...]) * (fac.shape[1] / n_all)
    mine = (
        pl.ds(pl.multiple_of(x * 128 + y * 32, 32), 32),
        pl.ds(pl.multiple_of(512 + y * 128 + x * 32, 32), 32),
    )
    k_final[mine[0], :] = k_small[1, 0:32]
    k_final[mine[1], :] = k_small[1, 32:64]
    for d in (1, 2, 3):
        start("k4", d - 1, k_small.at[1, 0:32, :], k_final.at[mine[0], :], dev(y=yp(d)))
        start("k4", d + 2, k_small.at[1, 32:64, :], k_final.at[mine[1], :], dev(x=xp(d)))
    for d in (1, 2, 3):
        at = pl.ds(pl.multiple_of(x * 128 + yp(-d) * 32, 32), 32)
        arrive("k4", d - 1, k_final.at[at, :])
        at = pl.ds(pl.multiple_of(512 + y * 128 + xp(-d) * 32, 32), 32)
        arrive("k4", d + 2, k_final.at[at, :])
    whole = lambda i: k_final.at[pl.ds(pl.multiple_of(i * 128, 128), 128), :]
    for d in (1, 2, 3):
        start("k5", d - 1, whole(x), whole(x), dev(x=xp(d)))
        start("k5", d + 2, whole(4 + y), whole(4 + y), dev(y=yp(d)))

    for d in (1, 2, 3):
        arrive("zr", d - 1, ring.at[zh * 4 + (zl - d + 4) % 4])
    for d in range(4):
        arrive("zr", d + 3, ring.at[(1 - zh) * 4 + (zl - d + 4) % 4])
    summed = ring[0]
    for i in range(1, 8):
        summed = summed + ring[i]
    total[1] = summed * (1.0 / math.sqrt(n_all * n_rel))
    start("fin", 0, total.at[1], total_in.at[h], sibling)
    total_in[h] = total[1]
    arrive("fin", 0, total_in.at[other])
    gf_ref[...] = total_in[...].reshape(gf_ref.shape).T

    for d in (1, 2, 3):
        arrive("k5", d - 1, whole(xp(-d)))
        arrive("k5", d + 2, whole(4 + yp(-d)))
    gc_ref[...] = k_final[...].reshape(gc_ref.shape)

    small = spread_f.at[0, 0, 0, 0]
    for d in range(3):
        sent("a1", d, small)
        sent("b1", d, small)
        sent("a2", d, column)
        sent("b2", d, column)
    for source, *targets in near:
        for i in range(len(targets)):
            @pl.when(zl == source)
            def _():
                sent("z", i, small)
    for t in range(8):
        sent("fwd", t, column)
        sent("swap", t, swapped.at[t])
    for i in range(6):
        sent("r1", i, r1_out.at[i])
        sent("r2", i, r2_in.at[i])
        sent("k1", i, k1_in.at[i])
        sent("k2", i, k2_in.at[i])
        sent("k4", i, k2_in.at[i])
        sent("k5", i, k1_in.at[i])
    for i in range(7):
        sent("zr", i, own_in)
    sent("own", 0, own_in)
    sent("fin", 0, own_in)
    sent("k3", 0, k3_in)


def per_device(facts, observed, factors, cores):
    n_rel, n_own, n_all = facts.shape
    rank = factors.shape[1]
    vmem = pltpu.VMEM
    anywhere = pl.BlockSpec(memory_space=pl.ANY)
    inside = pl.BlockSpec(memory_space=pltpu.VMEM)
    return pl.pallas_call(
        kernel,
        out_shape=(
            jax.ShapeDtypeStruct((n_own, rank), F32),
            jax.ShapeDtypeStruct((n_rel, rank, rank), F32),
        ),
        in_specs=[anywhere] * 4,
        out_specs=(inside, inside),
        scratch_shapes=[
            vmem(facts.shape, BF16),
            vmem(observed.shape, jnp.int32),
            vmem(factors.shape, BF16),
            vmem(cores.shape, BF16),
            vmem(facts.shape, BF16),
            vmem((n_rel * n_own, rank), BF16),
            vmem((rank, n_rel * n_own), BF16),
            vmem((n_rel * n_own, 512), BF16),
            vmem((n_rel * n_own, rank), F32),
            vmem((n_rel * n_own, rank), BF16),
            vmem((2, 4, 4, 2, 64, rank), BF16),
            vmem((8, rank, 512), F32),
            vmem((8, 64, 512), F32),
            vmem((2, 64, 512), F32),
            vmem((6, 64, 512), WIDE),
            vmem((6, 64, 512), WIDE),
            vmem((6, 64, 128), F32),
            vmem((8, 64, 128), F32),
            vmem((rank, n_own), F32),
            vmem((64, 128), F32),
            vmem((2, 64, 128), F32),
            vmem((2, 64, 128), F32),
            vmem((n_rel, rank, rank), F32),
            vmem((6, rank, rank), F32),
            vmem((2, rank, rank), F32),
            vmem((6, 32, rank), F32),
            vmem((2, 64, rank), F32),
            vmem((64, rank), F32),
            vmem((n_rel * rank, rank), F32),
            pltpu.SemaphoreType.DMA((4,)),
            pltpu.SemaphoreType.DMA((TOTAL,)),
            pltpu.SemaphoreType.DMA((TOTAL,)),
        ],
        compiler_params=pltpu.CompilerParams(
            collective_id=0, has_side_effects=True, vmem_limit_bytes=56 * 2**20
        ),
        cost_estimate=pl.CostEstimate(
            flops=6 * n_rel * n_own * n_all * rank,
            bytes_accessed=facts.size * 2 + observed.size * 4,
            transcendentals=0,
        ),
        name="rescal_gradients",
    )(facts, observed, factors, cores)


def solution(mesh):
    return jax.shard_map(
        per_device,
        mesh=mesh,
        in_specs=(
            P("rel", "ent", None),
            P("rel", "ent", None),
            P("ent", None),
            P("rel", None, None),
        ),
        out_specs=(P("ent", None), P("rel", None, None)),
        check_vma=False,
    )
```

```python
import math

import jax
import jax.numpy as jnp
from jax import lax
from jax.experimental import pallas as pl
from jax.experimental.pallas import tpu as pltpu
from jax.sharding import PartitionSpec as P

F32, BF16 = jnp.float32, jnp.bfloat16
MESH = pl.DeviceIdType.MESH
NT = (((1,), (1,)), ((), ()))
ROWS_TYPE = BF16
CORE_TYPE = F32

COUNTS = dict(a=15, b=15, z=2, fwd=8, swap=8, r1=30, zr=7, own=1, fin=1, k1=15, k3=1, k5=15)
BASE, TOTAL = {}, 0
for _name, _count in COUNTS.items():
    BASE[_name] = TOTAL
    TOTAL += _count

PLANE = sorted(
    ((dx, dy) for dx in range(4) for dy in range(4) if dx or dy),
    key=lambda d: -(min(d[0], 4 - d[0]) + min(d[1], 4 - d[1])),
)
SLOT = lambda dx, dy: dx * 4 + dy - 1
ORDER = (0, 1, 3, 2)
NEAR = ((0, 3, 2), (3, 0, 1))


def unpack(obs, mask, k, n_words):
    rows = obs.shape[0] // 8
    low_half = obs[pl.ds(k, rows, stride=8), :]
    high_half = obs[pl.ds(k + 4, rows, stride=8), :]
    both = jnp.bitwise_or(low_half, jnp.left_shift(high_half, 16))
    sources = [both[first : first + 128].T for first in range(0, rows, 128)]
    n_tiles = mask.shape[2] // 128
    lane = lax.broadcasted_iota(jnp.int32, (128, 128), 1)
    for q in range(13):
        column = lane + 128 * q
        word = (column * 5042) >> 16
        low = jnp.left_shift(1, column - word * 13)
        high = jnp.left_shift(low, 16)
        for period, source in enumerate(sources):
            tile = 13 * period + q
            if tile >= n_tiles:
                continue
            spread = jnp.take_along_axis(source, word, axis=1, mode="promise_in_bounds")
            at = slice(128 * tile, 128 * tile + 128)
            mask[k, :, at] = jnp.where((spread & low) != 0, 1.0, 0.0).astype(BF16)
            mask[k + 4, :, at] = jnp.where((spread & high) != 0, 1.0, 0.0).astype(BF16)


def kernel(
    facts_hbm, obs_hbm, fac_hbm, cores_hbm, gf_ref, gc_hbm,
    facts, obs, fac, cores, mask, left, left_t, err, pull, pull_hi, spread_f,
    blk, swapped, acc, r1_out, r1_in, ring, own, own_in, total, total_in,
    part, k1_out, k1_in, k_small, k3_in, k_final,
    local, send, recv,
):
    rel, ent = lax.axis_index("rel"), lax.axis_index("ent")
    zl, h = rel // 2, rel % 2
    x, zh, y = ent // 8, (ent // 4) % 2, ent % 4
    z = zh * 4 + zl
    other = 1 - h
    n_words = obs_hbm.shape[0] // 8

    def dev(x=x, y=y, zh=zh, zl=zl, c=h):
        return {"rel": zl * 2 + c, "ent": x * 8 + zh * 4 + y}

    near_x = lambda d: (x + d + 4) % 4
    near_y = lambda d: (y + d + 4) % 4
    sibling = dev(c=other)
    pending = []

    def message(kind, index, src, dst, to):
        at = BASE[kind] + index
        return pltpu.make_async_remote_copy(
            src_ref=src, dst_ref=dst, send_sem=send.at[at], recv_sem=recv.at[at],
            device_id=to, device_id_type=MESH,
        )

    def start(kind, index, src, dst, to, track=True):
        message(kind, index, src, dst, to).start()
        if track:
            pending.append((kind, index, src))

    def arrive(kind, index, dst):
        message(kind, index, dst, dst, sibling).wait_recv()

    def sent(kind, index, src):
        message(kind, index, src, src, sibling).wait_send()

    loads = [
        pltpu.make_async_copy(obs_hbm, obs.at[pl.ds(0, n_words * 8), :], local.at[1]),
        pltpu.make_async_copy(fac_hbm, fac, local.at[0]),
        pltpu.make_async_copy(cores_hbm, cores, local.at[2]),
        pltpu.make_async_copy(facts_hbm, facts, local.at[3]),
    ]
    for load in loads:
        load.start()
    barrier = pltpu.get_barrier_semaphore()
    greeted = (
        [dev(zh=(z + d) % 8 // 4, zl=(z + d) % 4) for d in range(1, 8)]
        + [dev(x=near_x(dx), y=near_y(dy)) for dx, dy in PLANE]
        + [sibling]
    )
    for device in greeted:
        pl.semaphore_signal(barrier, inc=1, device_id=device, device_id_type=MESH)

    obs[n_words * 8 :, :] = jnp.zeros((obs.shape[0] - n_words * 8, 128), jnp.int32)
    pull[...] = jnp.zeros_like(pull)
    loads[0].wait()

    def two_masks(k, carry):
        unpack(obs, mask, k, n_words)
        return carry

    lax.fori_loop(0, 4, two_masks, 0)
    loads[1].wait()
    half = pl.ds(pl.multiple_of(h * 64, 64), 64)
    other_half = pl.ds(pl.multiple_of(other * 64, 64), 64)
    spread_f[0, x, y, h] = fac[half, :]

    pl.semaphore_wait(barrier, len(greeted))

    for source, *targets in NEAR:
        @pl.when(zl == source)
        def _():
            for i, target in enumerate(targets):
                start(
                    "z", i, fac.at[half, :], spread_f.at[1, x, y, h],
                    dev(zh=1 - zh, zl=target), track=False,
                )
    for dx, dy in PLANE:
        start(
            "a", SLOT(dx, dy), fac.at[half, :], spread_f.at[0, x, y, h],
            dev(x=near_x(dx), y=near_y(dy)),
        )

    loads[2].wait()
    for k in range(cores.shape[0]):
        rows = slice(128 * k, 128 * k + 128)
        value = jnp.dot(fac[...], cores[k], preferred_element_type=F32)
        left[rows, :] = value.astype(BF16)
        left_t[:, rows] = value.T.astype(BF16)

    for source, *targets in NEAR:
        for i, target in enumerate(targets):
            @pl.when(zl == target)
            def _():
                arrive("z", i, spread_f.at[1, x, y, h])
    for dx, dy in PLANE:
        start(
            "b", SLOT(dx, dy), spread_f.at[1, x, y, h], spread_f.at[1, x, y, h],
            dev(x=near_x(dx), y=near_y(dy)),
        )

    def forward(kind, part_of):
        for u, dx in enumerate(ORDER):
            for dy in range(4):
                if dx or dy:
                    slot = SLOT((4 - dx) % 4, (4 - dy) % 4)
                    arrive(kind, slot, spread_f.at[part_of, near_x(dx), near_y(dy), h])
            group = spread_f.at[part_of, near_x(dx), :, h]
            start("fwd", part_of * 4 + u, group, group, sibling, track=part_of == 0)

    forward("a", 0)
    loads[3].wait()

    def place(t):
        part_of, u = t // 4, t % 4
        dx = u + (u // 2) * (5 - 2 * u)
        return part_of, dx, (x + dx) % 4

    def settle(t):
        part_of, dx, group = place(t)
        arrive("swap", t, swapped.at[t])
        terms = blk[t, half, :] + swapped[t]
        for j in range(4):
            r1_out[t, j] = terms[:, 128 * j : 128 * j + 128].astype(ROWS_TYPE)

        @pl.when(dx == 0)
        def _():
            lanes = pl.ds(pl.multiple_of(y * 128, 128), 128)
            acc[part_of] = blk[t, half, lanes] + swapped[t, :, lanes]

        def hand(dy):
            slot = part_of * 15 + dx * 4 + dy - 1
            start(
                "r1", slot, r1_out.at[t, near_y(dy)], r1_in.at[slot],
                dev(x=group, y=near_y(dy)), track=False,
            )

        for dy in (2, 1, 3):
            hand(dy)

        @pl.when(dx != 0)
        def _():
            hand(0)

    def step(t, carry):
        part_of, dx, group = place(t)

        @pl.when(t == 3)
        def _():
            forward("b", 1)

        arrive("fwd", t, spread_f.at[part_of, group, :, other])
        rows = spread_f[part_of, group].reshape(512, 128)
        columns = pl.ds(
            pl.multiple_of(group * 1024 + (zh + part_of * (1 - 2 * zh)) * 512, 512), 512
        )
        model = lax.dot_general(left[...], rows, NT, preferred_element_type=F32)
        for k in range(cores.shape[0]):
            here = slice(128 * k, 128 * k + 128)
            diff = model[here] - facts[k, :, columns].astype(F32)
            err[here, :] = diff.astype(BF16) * mask[k, :, columns]
        pull[...] += jnp.dot(err[...], rows, preferred_element_type=F32)
        blk[t] = jnp.dot(left_t[...], err[...], preferred_element_type=F32)
        start("swap", t, blk.at[t, other_half, :], swapped.at[t], sibling, track=False)

        @pl.when(t >= 1)
        def _():
            settle(t - 1)

        return carry

    lax.fori_loop(0, 8, step, 0)

    fac_t = fac[...].astype(F32).T.astype(BF16)
    pull_hi[...] = pull[...].astype(BF16)
    for k in range(cores.shape[0]):
        rows = slice(128 * k, 128 * k + 128)
        value = jnp.dot(fac_t, pull_hi[rows, :], preferred_element_type=F32)
        part[2 * k : 2 * k + 2] = value.reshape(2, 64, 128)
    k1_out[...] = part[...].astype(CORE_TYPE)
    chunk = x * 4 + y
    for dx, dy in PLANE:
        start(
            "k1", SLOT(dx, dy), k1_out.at[near_x(dx) * 4 + near_y(dy)],
            k1_in.at[SLOT(dx, dy)], dev(x=near_x(dx), y=near_y(dy)),
        )
    own_value = jnp.zeros((128, 128), F32)
    for k in range(cores.shape[0]):
        rows = slice(128 * k, 128 * k + 128)
        high = pull_hi[rows, :]
        low = (pull[rows, :] - high.astype(F32)).astype(BF16)
        own_value += lax.dot_general(cores[k], high, NT, preferred_element_type=F32)
        own_value += lax.dot_general(cores[k], low, NT, preferred_element_type=F32)
    own[...] = own_value
    start("own", 0, own.at[other_half, :], own_in, sibling)
    settle(7)

    value = part[chunk]
    for i in range(15):
        arrive("k1", i, k1_in.at[i])
        value = value + k1_in[i].astype(F32)
    k_small[0] = value
    start("k3", 0, k_small.at[0], k3_in, dev(zh=1 - zh))

    arrive("own", 0, own_in)
    sums = [acc[0] + own[half, :] + own_in[...], acc[1]]
    for i in range(30):
        arrive("r1", i, r1_in.at[i])
        sums[i // 15] = sums[i // 15] + r1_in[i].astype(F32)
    ring[z] = sums[0]
    total[0] = sums[1]
    for d in range(4):
        start("zr", d + 3, total.at[0], ring.at[z], dev(zh=1 - zh, zl=(zl + d) % 4))
    for d in (1, 2, 3):
        start("zr", d - 1, ring.at[z], ring.at[z], dev(zl=(zl + d) % 4))

    n_all = facts.shape[2]
    n_rel = cores.shape[0] * lax.axis_size("rel")
    arrive("k3", 0, k3_in)
    k_final[chunk] = (k_small[0] + k3_in[...]) * (fac.shape[1] / n_all)
    for dx, dy in PLANE:
        start(
            "k5", SLOT(dx, dy), k_final.at[chunk], k_final.at[chunk],
            dev(x=near_x(dx), y=near_y(dy)),
        )

    for d in (1, 2, 3):
        arrive("zr", d - 1, ring.at[zh * 4 + (zl - d + 4) % 4])
    for d in range(4):
        arrive("zr", d + 3, ring.at[(1 - zh) * 4 + (zl - d + 4) % 4])
    summed = ring[0]
    for i in range(1, 8):
        summed = summed + ring[i]
    total[1] = summed * (1.0 / math.sqrt(n_all * n_rel))
    start("fin", 0, total.at[1], total_in.at[h], sibling)
    total_in[h] = total[1]

    for dx, dy in PLANE:
        slot = SLOT((4 - dx) % 4, (4 - dy) % 4)
        arrive("k5", slot, k_final.at[near_x(dx) * 4 + near_y(dy)])
    store = pltpu.make_async_copy(k_final, gc_hbm, local.at[0])
    store.start()
    arrive("fin", 0, total_in.at[other])
    gf_ref[...] = total_in[...].reshape(gf_ref.shape).T

    for kind, index, src in pending:
        sent(kind, index, src)
    for source, *targets in NEAR:
        @pl.when(zl == source)
        def _():
            for i in range(len(targets)):
                sent("z", i, fac.at[half, :])
    for t in range(8):
        sent("swap", t, swapped.at[t])
    for i in range(4):
        sent("fwd", 4 + i, spread_f.at[1, 0, :, h])
    for i in range(30):
        sent("r1", i, r1_in.at[i])
    store.wait()


def deliver_kernel(gf_in, gc_in, gf_out, gc_out, gf, gc, sems):
    count = gc_in.shape[0] // 4
    pieces = [(gf_in, gf, gf_out)]
    for first in range(0, gc_in.shape[0], count):
        at = pl.ds(first, count)
        pieces.append((gc_in.at[at], gc.at[at], gc_out.at[at]))
    loads = [pltpu.make_async_copy(p[0], p[1], sems.at[0, i]) for i, p in enumerate(pieces)]
    stores = [pltpu.make_async_copy(p[1], p[2], sems.at[1, i]) for i, p in enumerate(pieces)]
    for load in loads:
        load.start()
    for load, store in zip(loads, stores):
        load.wait()
        store.start()
    for store in stores:
        store.wait()


def per_device(facts, observed, factors, cores):
    n_rel, n_own, n_all = facts.shape
    rank = factors.shape[1]
    vmem = pltpu.VMEM
    anywhere = pl.BlockSpec(memory_space=pl.ANY)
    inside = pl.BlockSpec(memory_space=pltpu.VMEM)
    n_words = observed.shape[2]
    words = jnp.transpose(observed, (2, 0, 1)).reshape(n_words * n_rel, n_own)
    half = rank // 2
    shapes = (
        jax.ShapeDtypeStruct((n_own, rank), F32),
        jax.ShapeDtypeStruct((2 * n_rel, half, rank), F32),
    )
    rows, cores_grad = pl.pallas_call(
        kernel,
        out_shape=shapes,
        in_specs=[anywhere] * 4,
        out_specs=(inside, anywhere),
        scratch_shapes=[
            vmem(facts.shape, BF16),
            vmem((pl.cdiv(n_words, 128) * 128 * n_rel, n_own), jnp.int32),
            vmem(factors.shape, BF16),
            vmem(cores.shape, BF16),
            vmem(facts.shape, BF16),
            vmem((n_rel * n_own, rank), BF16),
            vmem((rank, n_rel * n_own), BF16),
            vmem((n_rel * n_own, 512), BF16),
            vmem((n_rel * n_own, rank), F32),
            vmem((n_rel * n_own, rank), BF16),
            vmem((2, 4, 4, 2, half, rank), BF16),
            vmem((8, rank, 512), F32),
            vmem((8, half, 512), F32),
            vmem((2, half, 128), F32),
            vmem((8, 4, half, 128), ROWS_TYPE),
            vmem((30, half, 128), ROWS_TYPE),
            vmem((8, half, 128), F32),
            vmem((rank, n_own), F32),
            vmem((half, 128), F32),
            vmem((2, half, 128), F32),
            vmem((2, half, 128), F32),
            vmem((2 * n_rel, half, rank), F32),
            vmem((2 * n_rel, half, rank), CORE_TYPE),
            vmem((15, half, rank), CORE_TYPE),
            vmem((1, half, rank), F32),
            vmem((half, rank), F32),
            vmem((2 * n_rel, half, rank), F32),
            pltpu.SemaphoreType.DMA((4,)),
            pltpu.SemaphoreType.DMA((TOTAL,)),
            pltpu.SemaphoreType.DMA((TOTAL,)),
        ],
        compiler_params=pltpu.CompilerParams(
            collective_id=0, has_side_effects=True, vmem_limit_bytes=56 * 2**20
        ),
        cost_estimate=pl.CostEstimate(
            flops=6 * n_rel * n_own * n_all * rank,
            bytes_accessed=facts.size * 2 + observed.size * 4,
            transcendentals=0,
        ),
        name="rescal_gradients",
    )(facts, words, factors, cores)
    rows, cores_grad = pl.pallas_call(
        deliver_kernel,
        out_shape=shapes,
        in_specs=[anywhere] * 2,
        out_specs=(anywhere, anywhere),
        scratch_shapes=[
            vmem(shapes[0].shape, F32),
            vmem(shapes[1].shape, F32),
            pltpu.SemaphoreType.DMA((2, 5)),
        ],
        name="deliver",
    )(rows, cores_grad)
    return rows, cores_grad.reshape(n_rel, rank, rank)


def solution(mesh):
    return jax.shard_map(
        per_device,
        mesh=mesh,
        in_specs=(
            P("rel", "ent", None),
            P("rel", "ent", None),
            P("ent", None),
            P("rel", None, None),
        ),
        out_specs=(P("ent", None), P("rel", None, None)),
        check_vma=False,
    )
```

```python
import math

import jax
import jax.numpy as jnp
from jax import lax
from jax.experimental import pallas as pl
from jax.experimental.pallas import tpu as pltpu
from jax.sharding import PartitionSpec as P

F32, BF16 = jnp.float32, jnp.bfloat16
MESH = pl.DeviceIdType.MESH
NT = (((1,), (1,)), ((), ()))
ROWS_TYPE = BF16
CORE_TYPE = F32
EARLY = 4

COUNTS = dict(a=15, b=15, z=2, fwd=8, swap=8, r1=30, zr=7, own=1, fin=1, k1=15, k3=1, k5=15)
BASE, TOTAL = {}, 0
for _name, _count in COUNTS.items():
    BASE[_name] = TOTAL
    TOTAL += _count

PLANE = sorted(
    ((dx, dy) for dx in range(4) for dy in range(4) if dx or dy),
    key=lambda d: -(min(d[0], 4 - d[0]) + min(d[1], 4 - d[1])),
)
SLOT = lambda dx, dy: dx * 4 + dy - 1
ORDER = (0, 1, 3, 2)
NEAR = ((0, 3, 2), (3, 0, 1))


def unpack(obs, mask, k):
    rows = obs.shape[0] // 8
    low_half = obs[pl.ds(k, rows, stride=8), :]
    high_half = obs[pl.ds(k + 4, rows, stride=8), :]
    both = jnp.bitwise_or(low_half, jnp.left_shift(high_half, 16))
    sources = [both[first : first + 128].T for first in range(0, rows, 128)]
    n_tiles = mask.shape[2] // 128
    lane = lax.broadcasted_iota(jnp.int32, (128, 128), 1)
    for q in range(13):
        column = lane + 128 * q
        word = (column * 5042) >> 16
        low = jnp.left_shift(1, column - word * 13)
        high = jnp.left_shift(low, 16)
        for period, source in enumerate(sources):
            tile = 13 * period + q
            if tile >= n_tiles:
                continue
            spread = jnp.take_along_axis(source, word, axis=1, mode="promise_in_bounds")
            at = slice(128 * tile, 128 * tile + 128)
            mask[k, :, at] = jnp.where((spread & low) != 0, 1.0, 0.0).astype(BF16)
            mask[k + 4, :, at] = jnp.where((spread & high) != 0, 1.0, 0.0).astype(BF16)


def kernel(
    facts_hbm, obs_hbm, fac_hbm, cores_hbm, gf_hbm, gc_hbm,
    facts, obs, fac, cores, mask, left, left_t, err, pull, spread_f,
    blk, swapped, acc, r1_out, r1_in, ring, own, own_in, total, total_in,
    part, k1_out, k1_in, k_small, k3_in, k_final, result,
    local, send, recv,
):
    rel, ent = lax.axis_index("rel"), lax.axis_index("ent")
    zl, h = rel // 2, rel % 2
    x, zh, y = ent // 8, (ent // 4) % 2, ent % 4
    z = zh * 4 + zl
    other = 1 - h
    n_words = obs_hbm.shape[0] // 8

    def dev(x=x, y=y, zh=zh, zl=zl, c=h):
        return {"rel": zl * 2 + c, "ent": x * 8 + zh * 4 + y}

    near_x = lambda d: (x + d + 4) % 4
    near_y = lambda d: (y + d + 4) % 4
    sibling = dev(c=other)
    pending = []

    def message(kind, index, src, dst, to):
        at = BASE[kind] + index
        return pltpu.make_async_remote_copy(
            src_ref=src, dst_ref=dst, send_sem=send.at[at], recv_sem=recv.at[at],
            device_id=to, device_id_type=MESH,
        )

    def start(kind, index, src, dst, to, track=True):
        message(kind, index, src, dst, to).start()
        if track:
            pending.append((kind, index, src))

    def arrive(kind, index, dst):
        message(kind, index, dst, dst, sibling).wait_recv()

    def sent(kind, index, src):
        message(kind, index, src, src, sibling).wait_send()

    barrier = pltpu.get_barrier_semaphore()
    greeted = (
        [dev(zh=(z + d) % 8 // 4, zl=(z + d) % 4) for d in range(1, 8)]
        + [dev(x=near_x(dx), y=near_y(dy)) for dx, dy in PLANE]
        + [sibling]
    )
    for device in greeted:
        pl.semaphore_signal(barrier, inc=1, device_id=device, device_id_type=MESH)
    loads = [
        pltpu.make_async_copy(obs_hbm, obs.at[pl.ds(0, n_words * 8), :], local.at[1]),
        pltpu.make_async_copy(fac_hbm, fac, local.at[0]),
        pltpu.make_async_copy(cores_hbm, cores, local.at[2]),
        pltpu.make_async_copy(facts_hbm, facts, local.at[3]),
    ]
    for i in (1, 0, 2, 3):
        loads[i].start()

    obs[n_words * 8 :, :] = jnp.zeros((obs.shape[0] - n_words * 8, 128), jnp.int32)
    pull[...] = jnp.zeros_like(pull)
    loads[1].wait()
    half = pl.ds(pl.multiple_of(h * 64, 64), 64)
    other_half = pl.ds(pl.multiple_of(other * 64, 64), 64)
    spread_f[0, x, y, h] = fac[half, :]
    pl.semaphore_wait(barrier, len(greeted))

    for source, *targets in NEAR:
        @pl.when(zl == source)
        def _():
            for i, target in enumerate(targets):
                start(
                    "z", i, fac.at[half, :], spread_f.at[1, x, y, h],
                    dev(zh=1 - zh, zl=target), track=False,
                )
    for dx, dy in PLANE:
        start(
            "a", SLOT(dx, dy), fac.at[half, :], spread_f.at[0, x, y, h],
            dev(x=near_x(dx), y=near_y(dy)),
        )

    loads[0].wait()

    def two_masks(k, carry):
        unpack(obs, mask, k)
        return carry

    lax.fori_loop(0, EARLY, two_masks, 0)
    for source, *targets in NEAR:
        for i, target in enumerate(targets):
            @pl.when(zl == target)
            def _():
                arrive("z", i, spread_f.at[1, x, y, h])
    for dx, dy in PLANE:
        start(
            "b", SLOT(dx, dy), spread_f.at[1, x, y, h], spread_f.at[1, x, y, h],
            dev(x=near_x(dx), y=near_y(dy)),
        )

    lax.fori_loop(EARLY, 4, two_masks, 0)
    loads[2].wait()
    wide = jnp.concatenate([cores[k] for k in range(cores.shape[0])], axis=1)
    lefts = jnp.dot(fac[...], wide, preferred_element_type=F32)
    for k in range(cores.shape[0]):
        rows = slice(128 * k, 128 * k + 128)
        value = lefts[:, rows]
        left[rows, :] = value.astype(BF16)
        left_t[:, rows] = value.T.astype(BF16)

    def forward(kind, part_of):
        for u, dx in enumerate(ORDER):
            for dy in range(4):
                if dx or dy:
                    slot = SLOT((4 - dx) % 4, (4 - dy) % 4)
                    arrive(kind, slot, spread_f.at[part_of, near_x(dx), near_y(dy), h])
            group = spread_f.at[part_of, near_x(dx), :, h]
            start("fwd", part_of * 4 + u, group, group, sibling, track=part_of == 0)

    forward("a", 0)
    loads[3].wait()

    def place(t):
        part_of, u = t // 4, t % 4
        dx = u + (u // 2) * (5 - 2 * u)
        return part_of, dx, (x + dx) % 4

    def settle(t):
        part_of, dx, group = place(t)
        arrive("swap", t, swapped.at[t])
        terms = blk[t, half, :] + swapped[t]
        for j in range(4):
            r1_out[t, j] = terms[:, 128 * j : 128 * j + 128].astype(ROWS_TYPE)

        @pl.when(dx == 0)
        def _():
            lanes = pl.ds(pl.multiple_of(y * 128, 128), 128)
            acc[part_of] = blk[t, half, lanes] + swapped[t, :, lanes]

        def hand(dy):
            slot = part_of * 15 + dx * 4 + dy - 1
            start(
                "r1", slot, r1_out.at[t, near_y(dy)], r1_in.at[slot],
                dev(x=group, y=near_y(dy)), track=False,
            )

        for dy in (2, 1, 3):
            hand(dy)

        @pl.when(dx != 0)
        def _():
            hand(0)

    def pass_on(t):
        blk[t] = jnp.dot(left_t[...], err[t % 4], preferred_element_type=F32)
        start("swap", t, blk.at[t, other_half, :], swapped.at[t], sibling, track=False)

    def step(t, carry):
        part_of, dx, group = place(t)
        u = t % 4

        @pl.when(t == 3)
        def _():
            forward("b", 1)

        arrive("fwd", t, spread_f.at[part_of, group, :, other])
        rows = spread_f[part_of, group].reshape(512, 128)
        columns = pl.ds(
            pl.multiple_of(group * 1024 + (zh + part_of * (1 - 2 * zh)) * 512, 512), 512
        )
        model = lax.dot_general(left[...], rows, NT, preferred_element_type=F32)
        for k in range(cores.shape[0]):
            here = slice(128 * k, 128 * k + 128)
            diff = model[here] - facts[k, :, columns].astype(F32)
            err[u, here, :] = diff.astype(BF16) * mask[k, :, columns]
        pull[...] += jnp.dot(err[u], rows, preferred_element_type=F32)

        @pl.when(t < 4)
        def _():
            pass_on(t)

        @pl.when((t >= 1) & (t < 5))
        def _():
            settle(t - 1)

        return carry

    lax.fori_loop(0, 8, step, 0)

    fac_t = fac[...].astype(F32).T.astype(BF16)
    stack = lambda value: jnp.concatenate(
        [value[128 * k : 128 * k + 128] for k in range(cores.shape[0])], axis=1
    )
    pulls = stack(pull[...])
    high = pulls.astype(BF16)
    core_terms = jnp.dot(fac_t, high, preferred_element_type=F32)
    for k in range(cores.shape[0]):
        value = core_terms[:, 128 * k : 128 * k + 128].reshape(2, 64, 128)
        part[2 * k : 2 * k + 2] = value
        k1_out[2 * k : 2 * k + 2] = value.astype(CORE_TYPE)
    chunk = x * 4 + y
    for dx, dy in PLANE:
        start(
            "k1", SLOT(dx, dy), k1_out.at[near_x(dx) * 4 + near_y(dy)],
            k1_in.at[SLOT(dx, dy)], dev(x=near_x(dx), y=near_y(dy)),
        )
    low = (pulls - high.astype(F32)).astype(BF16)
    own[...] = lax.dot_general(
        jnp.concatenate([wide, wide], axis=1), jnp.concatenate([high, low], axis=1), NT,
        preferred_element_type=F32,
    )
    start("own", 0, own.at[other_half, :], own_in, sibling)

    def late(t, carry):
        pass_on(t)

        @pl.when(t >= 5)
        def _():
            settle(t - 1)

        return carry

    lax.fori_loop(4, 8, late, 0)
    settle(7)

    value = part[chunk]
    for i in range(15):
        arrive("k1", i, k1_in.at[i])
        value = value + k1_in[i].astype(F32)
    k_small[0] = value
    start("k3", 0, k_small.at[0], k3_in, dev(zh=1 - zh))

    arrive("own", 0, own_in)
    sums = [acc[0] + own[half, :] + own_in[...], acc[1]]
    for i in range(30):
        arrive("r1", i, r1_in.at[i])
        sums[i // 15] = sums[i // 15] + r1_in[i].astype(F32)
    ring[z] = sums[0]
    total[0] = sums[1]
    for d in range(4):
        start("zr", d + 3, total.at[0], ring.at[z], dev(zh=1 - zh, zl=(zl + d) % 4))
    for d in (1, 2, 3):
        start("zr", d - 1, ring.at[z], ring.at[z], dev(zl=(zl + d) % 4))

    n_all = facts.shape[2]
    n_rel = cores.shape[0] * lax.axis_size("rel")
    arrive("k3", 0, k3_in)
    k_final[...] = (k_small[0] + k3_in[...]) * (fac.shape[1] / n_all)
    for dx, dy in PLANE:
        start(
            "k5", SLOT(dx, dy), k_final, gc_hbm.at[chunk], dev(x=near_x(dx), y=near_y(dy)),
        )
    store = pltpu.make_async_copy(k_final, gc_hbm.at[chunk], local.at[0])
    store.start()

    for d in (1, 2, 3):
        arrive("zr", d - 1, ring.at[zh * 4 + (zl - d + 4) % 4])
    for d in range(4):
        arrive("zr", d + 3, ring.at[(1 - zh) * 4 + (zl - d + 4) % 4])
    summed = ring[0]
    for i in range(1, 8):
        summed = summed + ring[i]
    total[1] = summed * (1.0 / math.sqrt(n_all * n_rel))
    start("fin", 0, total.at[1], total_in.at[h], sibling)
    total_in[h] = total[1]

    arrive("fin", 0, total_in.at[other])
    result[...] = total_in[...].reshape(result.shape).T
    store_rows = pltpu.make_async_copy(result, gf_hbm, local.at[1])
    store_rows.start()

    for dx, dy in PLANE:
        slot = SLOT((4 - dx) % 4, (4 - dy) % 4)
        arrive("k5", slot, gc_hbm.at[near_x(dx) * 4 + near_y(dy)])

    for kind, index, src in pending:
        sent(kind, index, src)
    for source, *targets in NEAR:
        @pl.when(zl == source)
        def _():
            for i in range(len(targets)):
                sent("z", i, fac.at[half, :])
    for t in range(8):
        sent("swap", t, swapped.at[t])
    for i in range(4):
        sent("fwd", 4 + i, spread_f.at[1, 0, :, h])
    for i in range(30):
        sent("r1", i, r1_in.at[i])
    store.wait()
    store_rows.wait()


def per_device(facts, observed, factors, cores):
    n_rel, n_own, n_all = facts.shape
    rank = factors.shape[1]
    vmem = pltpu.VMEM
    anywhere = pl.BlockSpec(memory_space=pl.ANY)
    n_words = observed.shape[2]
    words = jnp.transpose(observed, (2, 0, 1)).reshape(n_words * n_rel, n_own)
    half = rank // 2
    shapes = (
        jax.ShapeDtypeStruct((n_own, rank), F32),
        jax.ShapeDtypeStruct((2 * n_rel, half, rank), F32),
    )
    rows, cores_grad = pl.pallas_call(
        kernel,
        out_shape=tuple(vmem(shape.shape, shape.dtype) for shape in shapes),
        in_specs=[anywhere] * 4,
        out_specs=(anywhere, anywhere),
        scratch_shapes=[
            vmem(facts.shape, BF16),
            vmem((pl.cdiv(n_words, 128) * 128 * n_rel, n_own), jnp.int32),
            vmem(factors.shape, BF16),
            vmem(cores.shape, BF16),
            vmem(facts.shape, BF16),
            vmem((n_rel * n_own, rank), BF16),
            vmem((rank, n_rel * n_own), BF16),
            vmem((4, n_rel * n_own, 512), BF16),
            vmem((n_rel * n_own, rank), F32),
            vmem((2, 4, 4, 2, half, rank), BF16),
            vmem((8, rank, 512), F32),
            vmem((8, half, 512), F32),
            vmem((2, half, 128), F32),
            vmem((8, 4, half, 128), ROWS_TYPE),
            vmem((30, half, 128), ROWS_TYPE),
            vmem((8, half, 128), F32),
            vmem((rank, n_own), F32),
            vmem((half, 128), F32),
            vmem((2, half, 128), F32),
            vmem((2, half, 128), F32),
            vmem((2 * n_rel, half, rank), F32),
            vmem((2 * n_rel, half, rank), CORE_TYPE),
            vmem((15, half, rank), CORE_TYPE),
            vmem((1, half, rank), F32),
            vmem((half, rank), F32),
            vmem((half, rank), F32),
            vmem((n_own, rank), F32),
            pltpu.SemaphoreType.DMA((4,)),
            pltpu.SemaphoreType.DMA((TOTAL,)),
            pltpu.SemaphoreType.DMA((TOTAL,)),
        ],
        compiler_params=pltpu.CompilerParams(
            collective_id=0, has_side_effects=True, vmem_limit_bytes=56 * 2**20
        ),
        cost_estimate=pl.CostEstimate(
            flops=6 * n_rel * n_own * n_all * rank,
            bytes_accessed=facts.size * 2 + observed.size * 4,
            transcendentals=0,
        ),
        name="rescal_gradients",
    )(facts, words, factors, cores)
    return rows, cores_grad.reshape(n_rel, rank, rank)


def solution(mesh):
    return jax.shard_map(
        per_device,
        mesh=mesh,
        in_specs=(
            P("rel", "ent", None),
            P("rel", "ent", None),
            P("ent", None),
            P("rel", None, None),
        ),
        out_specs=(P("ent", None), P("rel", None, None)),
        check_vma=False,
    )
```

```python
import math

import jax
import jax.numpy as jnp
from jax import lax
from jax.experimental import pallas as pl
from jax.experimental.pallas import tpu as pltpu
from jax.sharding import PartitionSpec as P

F32, BF16 = jnp.float32, jnp.bfloat16
MESH = pl.DeviceIdType.MESH
NT = (((1,), (1,)), ((), ()))
ROWS_TYPE = BF16
CORE_TYPE = BF16

COUNTS = dict(a=15, b=15, z=2, fwd=8, swap=8, r1=30, zr=7, own=1, fin=1, k1=15, k3=1, k5=15)
BASE, TOTAL = {}, 0
for _name, _count in COUNTS.items():
    BASE[_name] = TOTAL
    TOTAL += _count

PLANE = sorted(
    ((dx, dy) for dx in range(4) for dy in range(4) if dx or dy),
    key=lambda d: -(min(d[0], 4 - d[0]) + min(d[1], 4 - d[1])),
)
SLOT = lambda dx, dy: dx * 4 + dy - 1
ORDER = (0, 1, 3, 2)
NEAR = ((0, 3, 2), (3, 0, 1))


def unpack(obs, mask, k):
    rows = obs.shape[0] // 8
    low_half = obs[pl.ds(k, rows, stride=8), :]
    high_half = obs[pl.ds(k + 4, rows, stride=8), :]
    both = jnp.bitwise_or(low_half, jnp.left_shift(high_half, 16))
    sources = [both[first : first + 128].T for first in range(0, rows, 128)]
    n_tiles = mask.shape[2] // 128
    lane = lax.broadcasted_iota(jnp.int32, (128, 128), 1)
    for q in range(13):
        column = lane + 128 * q
        word = (column * 5042) >> 16
        low = jnp.left_shift(1, column - word * 13)
        high = jnp.left_shift(low, 16)
        for period, source in enumerate(sources):
            tile = 13 * period + q
            if tile >= n_tiles:
                continue
            spread = jnp.take_along_axis(source, word, axis=1, mode="promise_in_bounds")
            at = slice(128 * tile, 128 * tile + 128)
            mask[k, :, at] = jnp.where((spread & low) != 0, 1.0, 0.0).astype(BF16)
            mask[k + 4, :, at] = jnp.where((spread & high) != 0, 1.0, 0.0).astype(BF16)


def kernel(
    facts_hbm, obs_hbm, fac_hbm, cores_hbm, gf_hbm, gc_hbm,
    facts, obs, fac, cores, mask, left, left_t, err, pull, spread_f,
    blk, swapped, acc, r1_out, r1_in, ring, own, own_in, total, total_in,
    part, k1_out, k1_in, k_small, k3_in, k_final, result,
    local, send, recv,
):
    rel, ent = lax.axis_index("rel"), lax.axis_index("ent")
    zl, h = rel // 2, rel % 2
    x, zh, y = ent // 8, (ent // 4) % 2, ent % 4
    z = zh * 4 + zl
    other = 1 - h
    n_words = obs_hbm.shape[0] // 8

    def dev(x=x, y=y, zh=zh, zl=zl, c=h):
        return {"rel": zl * 2 + c, "ent": x * 8 + zh * 4 + y}

    near_x = lambda d: (x + d + 4) % 4
    near_y = lambda d: (y + d + 4) % 4
    sibling = dev(c=other)
    pending = []

    def message(kind, index, src, dst, to):
        at = BASE[kind] + index
        return pltpu.make_async_remote_copy(
            src_ref=src, dst_ref=dst, send_sem=send.at[at], recv_sem=recv.at[at],
            device_id=to, device_id_type=MESH,
        )

    def start(kind, index, src, dst, to, track=True):
        message(kind, index, src, dst, to).start()
        if track:
            pending.append((kind, index, src))

    def arrive(kind, index, dst):
        message(kind, index, dst, dst, sibling).wait_recv()

    def sent(kind, index, src):
        message(kind, index, src, src, sibling).wait_send()

    loads = [
        pltpu.make_async_copy(obs_hbm, obs.at[pl.ds(0, n_words * 8), :], local.at[1]),
        pltpu.make_async_copy(fac_hbm, fac, local.at[0]),
        pltpu.make_async_copy(cores_hbm, cores, local.at[2]),
        pltpu.make_async_copy(facts_hbm, facts, local.at[3]),
    ]
    loads[1].start()
    loads[0].start()
    barrier = pltpu.get_barrier_semaphore()
    greeted = (
        [dev(zh=(z + d) % 8 // 4, zl=(z + d) % 4) for d in range(1, 8)]
        + [dev(x=near_x(dx), y=near_y(dy)) for dx, dy in PLANE]
        + [sibling]
    )
    for device in greeted:
        pl.semaphore_signal(barrier, inc=1, device_id=device, device_id_type=MESH)
    loads[2].start()
    loads[3].start()

    obs[n_words * 8 :, :] = jnp.zeros((obs.shape[0] - n_words * 8, 128), jnp.int32)
    pull[...] = jnp.zeros_like(pull)
    loads[1].wait()
    half = pl.ds(pl.multiple_of(h * 64, 64), 64)
    other_half = pl.ds(pl.multiple_of(other * 64, 64), 64)
    spread_f[0, x, y, h] = fac[half, :]
    pl.semaphore_wait(barrier, len(greeted))

    for source, *targets in NEAR:
        @pl.when(zl == source)
        def _():
            for i, target in enumerate(targets):
                start(
                    "z", i, fac.at[half, :], spread_f.at[1, x, y, h],
                    dev(zh=1 - zh, zl=target), track=False,
                )
    for dx, dy in PLANE:
        start(
            "a", SLOT(dx, dy), fac.at[half, :], spread_f.at[0, x, y, h],
            dev(x=near_x(dx), y=near_y(dy)),
        )

    loads[0].wait()

    def two_masks(k, carry):
        unpack(obs, mask, k)
        return carry

    lax.fori_loop(0, 4, two_masks, 0)
    loads[2].wait()
    wide = jnp.concatenate([cores[k] for k in range(cores.shape[0])], axis=1)
    lefts = jnp.dot(fac[...], wide, preferred_element_type=F32)
    fac_t = fac[...].astype(F32).T.astype(BF16)
    for k in range(cores.shape[0]):
        rows = slice(128 * k, 128 * k + 128)
        value = lefts[:, rows]
        left[rows, :] = value.astype(BF16)
        left_t[:, rows] = value.T.astype(BF16)

    for source, *targets in NEAR:
        for i, target in enumerate(targets):
            @pl.when(zl == target)
            def _():
                arrive("z", i, spread_f.at[1, x, y, h])
    for dx, dy in PLANE:
        start(
            "b", SLOT(dx, dy), spread_f.at[1, x, y, h], spread_f.at[1, x, y, h],
            dev(x=near_x(dx), y=near_y(dy)),
        )

    def forward(kind, part_of):
        for u, dx in enumerate(ORDER):
            for dy in range(4):
                if dx or dy:
                    slot = SLOT((4 - dx) % 4, (4 - dy) % 4)
                    arrive(kind, slot, spread_f.at[part_of, near_x(dx), near_y(dy), h])
            group = spread_f.at[part_of, near_x(dx), :, h]
            start("fwd", part_of * 4 + u, group, group, sibling, track=part_of == 0)

    forward("a", 0)
    loads[3].wait()

    def place(t):
        part_of, u = t // 4, t % 4
        dx = u + (u // 2) * (5 - 2 * u)
        return part_of, dx, (x + dx) % 4

    def settle(t):
        part_of, dx, group = place(t)
        arrive("swap", t, swapped.at[t])
        terms = blk[t, half, :] + swapped[t]
        for j in range(4):
            r1_out[t, j] = terms[:, 128 * j : 128 * j + 128].astype(ROWS_TYPE)

        @pl.when(dx == 0)
        def _():
            lanes = pl.ds(pl.multiple_of(y * 128, 128), 128)
            acc[part_of] = blk[t, half, lanes] + swapped[t, :, lanes]

        def hand(dy):
            slot = part_of * 15 + dx * 4 + dy - 1
            start(
                "r1", slot, r1_out.at[t, near_y(dy)], r1_in.at[slot],
                dev(x=group, y=near_y(dy)), track=False,
            )

        for dy in (2, 1, 3):
            hand(dy)

        @pl.when(dx != 0)
        def _():
            hand(0)

    def pass_on(t):
        blk[t] = jnp.dot(left_t[...], err[t % 4], preferred_element_type=F32)
        start("swap", t, blk.at[t, other_half, :], swapped.at[t], sibling, track=False)

    def step(t, carry):
        part_of, dx, group = place(t)
        u = t % 4

        @pl.when(t == 3)
        def _():
            forward("b", 1)

        arrive("fwd", t, spread_f.at[part_of, group, :, other])
        rows = spread_f[part_of, group].reshape(512, 128)
        columns = pl.ds(
            pl.multiple_of(group * 1024 + (zh + part_of * (1 - 2 * zh)) * 512, 512), 512
        )
        model = lax.dot_general(left[...], rows, NT, preferred_element_type=F32)
        for k in range(cores.shape[0]):
            here = slice(128 * k, 128 * k + 128)
            diff = model[here] - facts[k, :, columns].astype(F32)
            err[u, here, :] = diff.astype(BF16) * mask[k, :, columns]
        pull[...] += jnp.dot(err[u], rows, preferred_element_type=F32)

        @pl.when(t < 4)
        def _():
            pass_on(t)

        @pl.when((t >= 1) & (t < 5))
        def _():
            settle(t - 1)

        return carry

    lax.fori_loop(0, 8, step, 0)

    stack = lambda value: jnp.concatenate(
        [value[128 * k : 128 * k + 128] for k in range(cores.shape[0])], axis=1
    )
    pulls = stack(pull[...])
    high = pulls.astype(BF16)
    core_terms = jnp.dot(fac_t, high, preferred_element_type=F32)
    for k in range(cores.shape[0]):
        value = core_terms[:, 128 * k : 128 * k + 128].reshape(2, 64, 128)
        part[2 * k : 2 * k + 2] = value
        if CORE_TYPE != F32:
            k1_out[2 * k : 2 * k + 2] = value.astype(CORE_TYPE)
    core_source = part if CORE_TYPE == F32 else k1_out
    chunk = x * 4 + y
    for dx, dy in PLANE:
        start(
            "k1", SLOT(dx, dy), core_source.at[near_x(dx) * 4 + near_y(dy)],
            k1_in.at[SLOT(dx, dy)], dev(x=near_x(dx), y=near_y(dy)),
        )
    def late_terms(t, carry):
        pass_on(t)
        return carry

    lax.fori_loop(4, 8, late_terms, 0)
    low = (pulls - high.astype(F32)).astype(BF16)
    own[...] = lax.dot_general(
        jnp.concatenate([wide, wide], axis=1), jnp.concatenate([high, low], axis=1), NT,
        preferred_element_type=F32,
    )
    start("own", 0, own.at[other_half, :], own_in, sibling)

    def late_settle(t, carry):
        settle(t)
        return carry

    lax.fori_loop(4, 8, late_settle, 0)

    arrive("own", 0, own_in)
    value = acc[0] + own[half, :] + own_in[...]
    for i in range(15):
        arrive("r1", i, r1_in.at[i])
        value = value + r1_in[i].astype(F32)
    ring[z] = value
    for d in (1, 2, 3):
        start("zr", d - 1, ring.at[z], ring.at[z], dev(zl=(zl + d) % 4))

    value = part[chunk]
    for i in range(15):
        arrive("k1", i, k1_in.at[i])
        value = value + k1_in[i].astype(F32)
    k_small[0] = value
    start("k3", 0, k_small.at[0], k3_in, dev(zh=1 - zh))

    value = acc[1]
    for i in range(15, 30):
        arrive("r1", i, r1_in.at[i])
        value = value + r1_in[i].astype(F32)
    total[0] = value
    for d in range(4):
        start("zr", d + 3, total.at[0], ring.at[z], dev(zh=1 - zh, zl=(zl + d) % 4))

    n_all = facts.shape[2]
    n_rel = cores.shape[0] * lax.axis_size("rel")
    arrive("k3", 0, k3_in)
    k_final[...] = (k_small[0] + k3_in[...]) * (fac.shape[1] / n_all)
    for dx, dy in PLANE:
        start(
            "k5", SLOT(dx, dy), k_final, gc_hbm.at[chunk], dev(x=near_x(dx), y=near_y(dy)),
        )
    store = pltpu.make_async_copy(k_final, gc_hbm.at[chunk], local.at[0])
    store.start()

    for d in (1, 2, 3):
        arrive("zr", d - 1, ring.at[zh * 4 + (zl - d + 4) % 4])
    for d in range(4):
        arrive("zr", d + 3, ring.at[(1 - zh) * 4 + (zl - d + 4) % 4])
    summed = ring[0]
    for i in range(1, 8):
        summed = summed + ring[i]
    total[1] = summed * (1.0 / math.sqrt(n_all * n_rel))
    start("fin", 0, total.at[1], total_in.at[h], sibling)
    total_in[h] = total[1]

    arrive("fin", 0, total_in.at[other])
    result[...] = total_in[...].reshape(result.shape).T
    store_rows = pltpu.make_async_copy(result, gf_hbm, local.at[1])
    store_rows.start()

    for kind, index, src in pending:
        if kind != "k5":
            sent(kind, index, src)
    for source, *targets in NEAR:
        @pl.when(zl == source)
        def _():
            for i in range(len(targets)):
                sent("z", i, fac.at[half, :])
    for t in range(8):
        sent("swap", t, swapped.at[t])
    for i in range(4):
        sent("fwd", 4 + i, spread_f.at[1, 0, :, h])
    for i in range(30):
        sent("r1", i, r1_in.at[i])

    for dx, dy in PLANE:
        slot = SLOT((4 - dx) % 4, (4 - dy) % 4)
        arrive("k5", slot, gc_hbm.at[near_x(dx) * 4 + near_y(dy)])

    for kind, index, src in pending:
        if kind == "k5":
            sent(kind, index, src)
    store.wait()
    store_rows.wait()


def per_device(facts, observed, factors, cores):
    n_rel, n_own, n_all = facts.shape
    rank = factors.shape[1]
    vmem = pltpu.VMEM
    anywhere = pl.BlockSpec(memory_space=pl.ANY)
    n_words = observed.shape[2]
    words = jnp.transpose(observed, (2, 0, 1)).reshape(n_words * n_rel, n_own)
    half = rank // 2
    shapes = (
        jax.ShapeDtypeStruct((n_own, rank), F32),
        jax.ShapeDtypeStruct((2 * n_rel, half, rank), F32),
    )
    rows, cores_grad = pl.pallas_call(
        kernel,
        out_shape=tuple(vmem(shape.shape, shape.dtype) for shape in shapes),
        in_specs=[anywhere] * 4,
        out_specs=(anywhere, anywhere),
        scratch_shapes=[
            vmem(facts.shape, BF16),
            vmem((pl.cdiv(n_words, 128) * 128 * n_rel, n_own), jnp.int32),
            vmem(factors.shape, BF16),
            vmem(cores.shape, BF16),
            vmem(facts.shape, BF16),
            vmem((n_rel * n_own, rank), BF16),
            vmem((rank, n_rel * n_own), BF16),
            vmem((4, n_rel * n_own, 512), BF16),
            vmem((n_rel * n_own, rank), F32),
            vmem((2, 4, 4, 2, half, rank), BF16),
            vmem((8, rank, 512), F32),
            vmem((8, half, 512), F32),
            vmem((2, half, 128), F32),
            vmem((8, 4, half, 128), ROWS_TYPE),
            vmem((30, half, 128), ROWS_TYPE),
            vmem((8, half, 128), F32),
            vmem((rank, n_own), F32),
            vmem((half, 128), F32),
            vmem((2, half, 128), F32),
            vmem((2, half, 128), F32),
            vmem((2 * n_rel, half, rank), F32),
            vmem((2 * n_rel, half, rank), CORE_TYPE),
            vmem((15, half, rank), CORE_TYPE),
            vmem((1, half, rank), F32),
            vmem((half, rank), F32),
            vmem((half, rank), F32),
            vmem((n_own, rank), F32),
            pltpu.SemaphoreType.DMA((4,)),
            pltpu.SemaphoreType.DMA((TOTAL,)),
            pltpu.SemaphoreType.DMA((TOTAL,)),
        ],
        compiler_params=pltpu.CompilerParams(
            collective_id=0, has_side_effects=True, vmem_limit_bytes=56 * 2**20
        ),
        cost_estimate=pl.CostEstimate(
            flops=6 * n_rel * n_own * n_all * rank,
            bytes_accessed=facts.size * 2 + observed.size * 4,
            transcendentals=0,
        ),
        name="rescal_gradients",
    )(facts, words, factors, cores)
    return rows, cores_grad.reshape(n_rel, rank, rank)


def solution(mesh):
    return jax.shard_map(
        per_device,
        mesh=mesh,
        in_specs=(
            P("rel", "ent", None),
            P("rel", "ent", None),
            P("ent", None),
            P("rel", None, None),
        ),
        out_specs=(P("ent", None), P("rel", None, None)),
        check_vma=False,
    )
```

```python
import math

import jax
import jax.numpy as jnp
from jax import lax
from jax.experimental import pallas as pl
from jax.experimental.pallas import tpu as pltpu
from jax.sharding import PartitionSpec as P

F32, BF16 = jnp.float32, jnp.bfloat16
MESH = pl.DeviceIdType.MESH
NT = (((1,), (1,)), ((), ()))
ROWS_TYPE = BF16
CORE_TYPE = BF16

COUNTS = dict(a=15, b=15, z=2, fwd=8, swap=8, r1=30, zr=7, own=1, fin=1, k1=15, k3=1, k5=15)
BASE, TOTAL = {}, 0
for _name, _count in COUNTS.items():
    BASE[_name] = TOTAL
    TOTAL += _count

PLANE = sorted(
    ((dx, dy) for dx in range(4) for dy in range(4) if dx or dy),
    key=lambda d: -(min(d[0], 4 - d[0]) + min(d[1], 4 - d[1])),
)
SLOT = lambda dx, dy: dx * 4 + dy - 1
ORDER = (0, 1, 3, 2)
NEAR = ((0, 3, 2), (3, 0, 1))


def unpack(obs, mask, k):
    rows = obs.shape[0] // 8
    low_half = obs[pl.ds(k, rows, stride=8), :]
    high_half = obs[pl.ds(k + 4, rows, stride=8), :]
    both = jnp.bitwise_or(low_half, jnp.left_shift(high_half, 16))
    sources = [both[first : first + 128].T for first in range(0, rows, 128)]
    n_tiles = mask.shape[2] // 128
    lane = lax.broadcasted_iota(jnp.int32, (128, 128), 1)
    for q in range(13):
        column = lane + 128 * q
        word = (column * 5042) >> 16
        low = jnp.left_shift(1, column - word * 13)
        high = jnp.left_shift(low, 16)
        for period, source in enumerate(sources):
            tile = 13 * period + q
            if tile >= n_tiles:
                continue
            spread = jnp.take_along_axis(source, word, axis=1, mode="promise_in_bounds")
            at = slice(128 * tile, 128 * tile + 128)
            mask[k, :, at] = jnp.where((spread & low) != 0, 1.0, 0.0).astype(BF16)
            mask[k + 4, :, at] = jnp.where((spread & high) != 0, 1.0, 0.0).astype(BF16)


def kernel(
    facts_hbm, obs_hbm, fac_hbm, cores_hbm, gf_hbm, gc_hbm,
    facts, obs, fac, cores, mask, left, left_t, err, pull, spread_f,
    blk, swapped, acc, r1_out, r1_in, ring, own, own_in, total, total_in,
    part, k1_out, k1_in, k_small, k3_in, k_final, result,
    local, send, recv,
):
    rel, ent = lax.axis_index("rel"), lax.axis_index("ent")
    zl, h = rel // 2, rel % 2
    x, zh, y = ent // 8, (ent // 4) % 2, ent % 4
    z = zh * 4 + zl
    other = 1 - h
    n_words = obs_hbm.shape[0] // 8

    def dev(x=x, y=y, zh=zh, zl=zl, c=h):
        return {"rel": zl * 2 + c, "ent": x * 8 + zh * 4 + y}

    near_x = lambda d: (x + d + 4) % 4
    near_y = lambda d: (y + d + 4) % 4
    sibling = dev(c=other)
    pending = []

    def message(kind, index, src, dst, to):
        at = BASE[kind] + index
        return pltpu.make_async_remote_copy(
            src_ref=src, dst_ref=dst, send_sem=send.at[at], recv_sem=recv.at[at],
            device_id=to, device_id_type=MESH,
        )

    def start(kind, index, src, dst, to, track=True):
        message(kind, index, src, dst, to).start()
        if track:
            pending.append((kind, index, src))

    def arrive(kind, index, dst):
        message(kind, index, dst, dst, sibling).wait_recv()

    def sent(kind, index, src):
        message(kind, index, src, src, sibling).wait_send()

    loads = [
        pltpu.make_async_copy(obs_hbm, obs.at[pl.ds(0, n_words * 8), :], local.at[1]),
        pltpu.make_async_copy(fac_hbm, fac, local.at[0]),
        pltpu.make_async_copy(cores_hbm, cores, local.at[2]),
        pltpu.make_async_copy(facts_hbm, facts, local.at[3]),
    ]
    loads[1].start()
    loads[0].start()
    barrier = pltpu.get_barrier_semaphore()
    greeted = (
        [dev(zh=(z + d) % 8 // 4, zl=(z + d) % 4) for d in range(1, 8)]
        + [dev(x=near_x(dx), y=near_y(dy)) for dx, dy in PLANE]
        + [sibling]
    )
    for device in greeted:
        pl.semaphore_signal(barrier, inc=1, device_id=device, device_id_type=MESH)
    loads[2].start()
    loads[3].start()

    obs[n_words * 8 :, :] = jnp.zeros((obs.shape[0] - n_words * 8, 128), jnp.int32)
    pull[...] = jnp.zeros_like(pull)
    loads[1].wait()
    half = pl.ds(pl.multiple_of(h * 64, 64), 64)
    other_half = pl.ds(pl.multiple_of(other * 64, 64), 64)
    spread_f[0, x, y, h] = fac[half, :]
    pl.semaphore_wait(barrier, len(greeted))

    for source, *targets in NEAR:
        @pl.when(zl == source)
        def _():
            for i, target in enumerate(targets):
                start(
                    "z", i, fac.at[half, :], spread_f.at[1, x, y, h],
                    dev(zh=1 - zh, zl=target), track=False,
                )
    for dx, dy in PLANE:
        start(
            "a", SLOT(dx, dy), fac.at[half, :], spread_f.at[0, x, y, h],
            dev(x=near_x(dx), y=near_y(dy)),
        )

    loads[0].wait()

    def two_masks(k, carry):
        unpack(obs, mask, k)
        return carry

    lax.fori_loop(0, 4, two_masks, 0)
    loads[2].wait()
    wide = jnp.concatenate([cores[k] for k in range(cores.shape[0])], axis=1)
    lefts = jnp.dot(fac[...], wide, preferred_element_type=F32)
    fac_t = fac[...].astype(F32).T.astype(BF16)
    for k in range(cores.shape[0]):
        rows = slice(128 * k, 128 * k + 128)
        value = lefts[:, rows]
        left[rows, :] = value.astype(BF16)
        left_t[:, rows] = value.T.astype(BF16)

    for source, *targets in NEAR:
        for i, target in enumerate(targets):
            @pl.when(zl == target)
            def _():
                arrive("z", i, spread_f.at[1, x, y, h])
    for dx, dy in PLANE:
        start(
            "b", SLOT(dx, dy), spread_f.at[1, x, y, h], spread_f.at[1, x, y, h],
            dev(x=near_x(dx), y=near_y(dy)),
        )

    def forward(kind, part_of):
        for u, dx in enumerate(ORDER):
            for dy in range(4):
                if dx or dy:
                    slot = SLOT((4 - dx) % 4, (4 - dy) % 4)
                    arrive(kind, slot, spread_f.at[part_of, near_x(dx), near_y(dy), h])
            group = spread_f.at[part_of, near_x(dx), :, h]
            start("fwd", part_of * 4 + u, group, group, sibling, track=part_of == 0)

    forward("a", 0)
    loads[3].wait()

    def place(t):
        part_of, u = t // 4, t % 4
        dx = u + (u // 2) * (5 - 2 * u)
        return part_of, dx, (x + dx) % 4

    def settle(t):
        part_of, dx, group = place(t)
        arrive("swap", t, swapped.at[t])
        terms = blk[t, half, :] + swapped[t]
        for j in range(4):
            r1_out[t, j] = terms[:, 128 * j : 128 * j + 128].astype(ROWS_TYPE)

        @pl.when(dx == 0)
        def _():
            lanes = pl.ds(pl.multiple_of(y * 128, 128), 128)
            acc[part_of] = blk[t, half, lanes] + swapped[t, :, lanes]

        def hand(dy):
            slot = part_of * 15 + dx * 4 + dy - 1
            start(
                "r1", slot, r1_out.at[t, near_y(dy)], r1_in.at[slot],
                dev(x=group, y=near_y(dy)), track=False,
            )

        for dy in (2, 1, 3):
            hand(dy)

        @pl.when(dx != 0)
        def _():
            hand(0)

    def pass_on(t):
        blk[t] = jnp.dot(left_t[...], err[t % 4], preferred_element_type=F32)
        start("swap", t, blk.at[t, other_half, :], swapped.at[t], sibling, track=False)

    def step(t, carry):
        part_of, dx, group = place(t)
        u = t % 4

        @pl.when(t == 3)
        def _():
            forward("b", 1)

        arrive("fwd", t, spread_f.at[part_of, group, :, other])
        rows = spread_f[part_of, group].reshape(512, 128)
        columns = pl.ds(
            pl.multiple_of(group * 1024 + (zh + part_of * (1 - 2 * zh)) * 512, 512), 512
        )
        model = lax.dot_general(left[...], rows, NT, preferred_element_type=F32)
        for k in range(cores.shape[0]):
            here = slice(128 * k, 128 * k + 128)
            diff = model[here] - facts[k, :, columns].astype(F32)
            err[u, here, :] = diff.astype(BF16) * mask[k, :, columns]
        pull[...] += jnp.dot(err[u], rows, preferred_element_type=F32)

        @pl.when(t < 4)
        def _():
            pass_on(t)

        @pl.when((t >= 1) & (t < 5))
        def _():
            settle(t - 1)

        return carry

    lax.fori_loop(0, 8, step, 0)

    stack = lambda value: jnp.concatenate(
        [value[128 * k : 128 * k + 128] for k in range(cores.shape[0])], axis=1
    )
    pulls = stack(pull[...])
    high = pulls.astype(BF16)
    core_terms = jnp.dot(fac_t, high, preferred_element_type=F32)
    for k in range(cores.shape[0]):
        value = core_terms[:, 128 * k : 128 * k + 128].reshape(2, 64, 128)
        part[2 * k : 2 * k + 2] = value
        if CORE_TYPE != F32:
            k1_out[2 * k : 2 * k + 2] = value.astype(CORE_TYPE)
    core_source = part if CORE_TYPE == F32 else k1_out
    chunk = x * 4 + y
    for dx, dy in PLANE:
        start(
            "k1", SLOT(dx, dy), core_source.at[near_x(dx) * 4 + near_y(dy)],
            k1_in.at[SLOT(dx, dy)], dev(x=near_x(dx), y=near_y(dy)),
        )
    def late_terms(t, carry):
        pass_on(11 - t)
        return carry

    lax.fori_loop(4, 8, late_terms, 0)
    low = (pulls - high.astype(F32)).astype(BF16)
    own[...] = lax.dot_general(
        jnp.concatenate([wide, wide], axis=1), jnp.concatenate([high, low], axis=1), NT,
        preferred_element_type=F32,
    )
    start("own", 0, own.at[other_half, :], own_in, sibling)

    def late_settle(t, carry):
        settle(11 - t)
        return carry

    lax.fori_loop(4, 8, late_settle, 0)

    arrive("own", 0, own_in)
    value = acc[0] + own[half, :] + own_in[...]
    for i in range(15):
        arrive("r1", i, r1_in.at[i])
        value = value + r1_in[i].astype(F32)
    ring[z] = value
    for d in (1, 2, 3):
        start("zr", d - 1, ring.at[z], ring.at[z], dev(zl=(zl + d) % 4))

    value = part[chunk]
    for i in range(15):
        arrive("k1", i, k1_in.at[i])
        value = value + k1_in[i].astype(F32)
    k_small[0] = value
    start("k3", 0, k_small.at[0], k3_in, dev(zh=1 - zh))

    value = acc[1]
    for i in range(15, 30):
        arrive("r1", i, r1_in.at[i])
        value = value + r1_in[i].astype(F32)
    total[0] = value
    for d in range(4):
        start("zr", d + 3, total.at[0], ring.at[z], dev(zh=1 - zh, zl=(zl + d) % 4))

    n_all = facts.shape[2]
    n_rel = cores.shape[0] * lax.axis_size("rel")
    arrive("k3", 0, k3_in)
    k_final[...] = (k_small[0] + k3_in[...]) * (fac.shape[1] / n_all)
    for dx, dy in PLANE:
        start(
            "k5", SLOT(dx, dy), k_final, gc_hbm.at[chunk], dev(x=near_x(dx), y=near_y(dy)),
        )
    store = pltpu.make_async_copy(k_final, gc_hbm.at[chunk], local.at[0])
    store.start()

    for d in (1, 2, 3):
        arrive("zr", d - 1, ring.at[zh * 4 + (zl - d + 4) % 4])
    for d in range(4):
        arrive("zr", d + 3, ring.at[(1 - zh) * 4 + (zl - d + 4) % 4])
    summed = ring[0]
    for i in range(1, 8):
        summed = summed + ring[i]
    total[1] = summed * (1.0 / math.sqrt(n_all * n_rel))
    start("fin", 0, total.at[1], total_in.at[h], sibling)
    total_in[h] = total[1]

    arrive("fin", 0, total_in.at[other])
    result[...] = total_in[...].reshape(result.shape).T
    store_rows = pltpu.make_async_copy(result, gf_hbm, local.at[1])
    store_rows.start()

    for kind, index, src in pending:
        if kind != "k5":
            sent(kind, index, src)
    for source, *targets in NEAR:
        @pl.when(zl == source)
        def _():
            for i in range(len(targets)):
                sent("z", i, fac.at[half, :])
    for t in range(8):
        sent("swap", t, swapped.at[t])
    for i in range(4):
        sent("fwd", 4 + i, spread_f.at[1, 0, :, h])
    for i in range(30):
        sent("r1", i, r1_in.at[i])

    for dx, dy in PLANE:
        slot = SLOT((4 - dx) % 4, (4 - dy) % 4)
        arrive("k5", slot, gc_hbm.at[near_x(dx) * 4 + near_y(dy)])

    for kind, index, src in pending:
        if kind == "k5":
            sent(kind, index, src)
    store.wait()
    store_rows.wait()


def per_device(facts, observed, factors, cores):
    n_rel, n_own, n_all = facts.shape
    rank = factors.shape[1]
    vmem = pltpu.VMEM
    anywhere = pl.BlockSpec(memory_space=pl.ANY)
    n_words = observed.shape[2]
    words = jnp.transpose(observed, (2, 0, 1)).reshape(n_words * n_rel, n_own)
    half = rank // 2
    shapes = (
        jax.ShapeDtypeStruct((n_own, rank), F32),
        jax.ShapeDtypeStruct((2 * n_rel, half, rank), F32),
    )
    rows, cores_grad = pl.pallas_call(
        kernel,
        out_shape=tuple(vmem(shape.shape, shape.dtype) for shape in shapes),
        in_specs=[anywhere] * 4,
        out_specs=(anywhere, anywhere),
        scratch_shapes=[
            vmem(facts.shape, BF16),
            vmem((pl.cdiv(n_words, 128) * 128 * n_rel, n_own), jnp.int32),
            vmem(factors.shape, BF16),
            vmem(cores.shape, BF16),
            vmem(facts.shape, BF16),
            vmem((n_rel * n_own, rank), BF16),
            vmem((rank, n_rel * n_own), BF16),
            vmem((4, n_rel * n_own, 512), BF16),
            vmem((n_rel * n_own, rank), F32),
            vmem((2, 4, 4, 2, half, rank), BF16),
            vmem((8, rank, 512), F32),
            vmem((8, half, 512), F32),
            vmem((2, half, 128), F32),
            vmem((8, 4, half, 128), ROWS_TYPE),
            vmem((30, half, 128), ROWS_TYPE),
            vmem((8, half, 128), F32),
            vmem((rank, n_own), F32),
            vmem((half, 128), F32),
            vmem((2, half, 128), F32),
            vmem((2, half, 128), F32),
            vmem((2 * n_rel, half, rank), F32),
            vmem((2 * n_rel, half, rank), CORE_TYPE),
            vmem((15, half, rank), CORE_TYPE),
            vmem((1, half, rank), F32),
            vmem((half, rank), F32),
            vmem((half, rank), F32),
            vmem((n_own, rank), F32),
            pltpu.SemaphoreType.DMA((4,)),
            pltpu.SemaphoreType.DMA((TOTAL,)),
            pltpu.SemaphoreType.DMA((TOTAL,)),
        ],
        compiler_params=pltpu.CompilerParams(
            collective_id=0, has_side_effects=True, vmem_limit_bytes=56 * 2**20
        ),
        cost_estimate=pl.CostEstimate(
            flops=6 * n_rel * n_own * n_all * rank,
            bytes_accessed=facts.size * 2 + observed.size * 4,
            transcendentals=0,
        ),
        name="rescal_gradients",
    )(facts, words, factors, cores)
    return rows, cores_grad.reshape(n_rel, rank, rank)


def solution(mesh):
    return jax.shard_map(
        per_device,
        mesh=mesh,
        in_specs=(
            P("rel", "ent", None),
            P("rel", "ent", None),
            P("ent", None),
            P("rel", None, None),
        ),
        out_specs=(P("ent", None), P("rel", None, None)),
        check_vma=False,
    )
```
